32 devices in a mesh: grp: 4 (over y, x), blk: 8 (over z, core).
Axes of the slice: x: 2, y: 2, z: 4, core: 2. Of those that a mesh axis runs over, the one named last changes fastest.
Arguments:
- feats: bfloat16 [32768, 256], P(('grp', 'blk')), may hold values from -6 to 6
- weight: bfloat16 [256, 256], replicated, may hold values from -0.375 to 0.375
- cotangent: bfloat16 [32768, 256], P(('grp', 'blk')), may hold values from -6 to 6
- labels: int32 [32768], P(('grp', 'blk')), may hold values from -86 to 171
- tile_vals: bfloat16 [4, 8, 8, 32, 128, 128], P('grp', 'blk'), may hold values from -0.09375 to 0.09375
- tile_row: int32 [4, 8, 8, 32], P('grp', 'blk'), may hold values from 0 to 7
- tile_col: int32 [4, 8, 8, 32], P('grp', 'blk'), may hold values from 0 to 7
- tile_count: int32 [4, 8, 8], P('grp', 'blk'), may hold values from 1 to 32, as said below
- hub_vals: bfloat16 [4, 8, 16, 128, 128], P('grp', 'blk'), may hold values from -0.09375 to 0.09375
- hub_col: int32 [4, 8, 16], P('grp', 'blk'), may hold values from 0 to 7
- hub_dest: int32 [4, 8, 16, 1], P(None, 'blk'), may hold values from 0 to 3; in each aligned block of 16 rows (0 to 15, 16 to 31, ..., all dimensions but the last counted through in order) at most 4 rows name the same one
- hub_row: int32 [4, 8, 16], P(None, 'blk'), may hold values from 0 to 7
Outputs:
- layer_out: bfloat16 [32768, 256], P(('grp', 'blk'))
- grad_feats: bfloat16 [32768, 256], P(('grp', 'blk'))
- grad_weight: float32 [256, 256], replicated
The draws below stay inside these ranges and needn't reach their ends.
Inputs may be any that keep to these rules, and one draw needn't show every extreme that they name: Only the first tile_count slots of a device's list for a source block are used; some device uses all 32. `hub_dest`: at most 4 of the 16 hub tiles of one device name the same group, and exactly 4 in some devices.
All inputs are finite; a program needn't handle non-finite values.
Results may differ from the reference program's by a relative error of at most 0.007.
Values may be sent and summed in bfloat16 or wider, within the bound.
No kernel may reach another device: no remote copies, remote signals or barrier semaphores. Data moves between devices by JAX's collectives and lax.ppermute only.
A program may use at most 192 MiB of HBM per device.

```python
import math
import jax
import jax.numpy as jnp
import numpy as np
from jax import lax

F = 256
TILE = 128
RT = 8
TPB = 32
HUB = 16
CAP = 4
NODES = 32768
N_GRP = 4
N_BLK = 8


def draw_tile_count(key, part):
    total = N_GRP * N_BLK * N_BLK
    base = jax.random.randint(key, (total,), max(1, TPB // 4), TPB + 1)
    where = jax.random.randint(jax.random.fold_in(key, 7), (), 0, total)
    filled = jnp.where(jnp.arange(total) == where, TPB, base)
    return filled.reshape(N_GRP, N_BLK, N_BLK).astype(jnp.int32)


def plant(values, stream_key, low, largest):
    shape = values.shape
    place = [jax.random.randint(jax.random.fold_in(stream_key, axis), (), 0, shape[axis]) for axis in range(len(shape))]
    values = values.at[tuple(place)].set(low)
    longest = shape.index(max(shape))
    place[longest] = (place[longest] + 1) % shape[longest]
    return values.at[tuple(place)].set(largest)


def steps_of(key, shape, cuts, smallest, top_value):
    level, own = 1.0, jax.random.fold_in(key, 6)
    for dim, parts in cuts:
        steps = jnp.exp(jax.random.uniform(jax.random.fold_in(own, dim), (parts,), jnp.float32, smallest / len(cuts), top_value / len(cuts)))
        level = level * jnp.repeat(steps, shape[dim] // parts).reshape([-1 if axis == dim else 1 for axis in range(len(shape))])
    return level


def assign_block(key, own, number, rows, amount, top, reach, lean):
    sequence = jax.random.permutation(key, amount)
    crowded, common = shares(amount, rows * top, reach, lean, True), shares(amount, rows * top, reach, lean, False)
    places = jnp.arange(amount)

    def named(tallies, rotation):
        used = int((tallies > 0).sum())
        fixed = max(1, used // 4)
        passed = fixed + (places - fixed + rotation * (used - fixed)) % max(1, amount - fixed)
        return jnp.zeros((amount,), jnp.int32).at[sequence[jnp.where(places < fixed, places, passed)]].set(jnp.asarray(tallies, jnp.int32))

    tallies = jnp.where(number % 4 == 0, named(crowded, number // 4), named(common, number - number // 4 - 1))
    mixed = jax.random.permutation(jax.random.fold_in(own, 3), amount)
    donor, taker = mixed[0:amount // 2 * 2:2], mixed[1:amount // 2 * 2:2]
    slack = jnp.minimum(tallies[donor] - 1, reach - tallies[taker]) // 2
    slack = jnp.where((donor == sequence[0]) | (taker == sequence[0]) | (tallies[taker] == 0), 0, jnp.maximum(slack, 0))
    passed = jax.random.randint(jax.random.fold_in(own, 4), (amount // 2,), 0, 1 << 20) % (slack + 1)
    tallies = tallies.at[donor].add(-passed).at[taker].add(passed)
    members = jnp.searchsorted(jnp.cumsum(tallies), jnp.arange(rows * top), side="right").astype(jnp.int32)
    listing = members.reshape(top, rows).T
    listing = listing[jax.random.permutation(jax.random.fold_in(own, 1), rows)]
    rotation = jax.random.randint(jax.random.fold_in(own, 2), (rows, 1), 0, top)
    return jnp.take_along_axis(listing, (jnp.arange(top)[None, :] + rotation) % top, axis=1)


def shares(count, total, reach, skew, full):
    weights = [(1 << 20) // math.isqrt(rank ** skew) + 1 for rank in range(1, count + 1)]
    largest = reach if full else min(reach, max(-(-total // count), total * weights[0] // sum(weights)))
    least = 1 if total - largest >= count - 1 else 0
    counts, surplus = [largest] + [least] * (count - 1), total - largest - least * (count - 1)
    while surplus > 0:
        free = [i for i in range(1, count) if counts[i] < largest] or [i for i in range(1, count) if counts[i] < reach]
        mass, left = sum([weights[i] for i in free]), surplus
        for i in free:
            more = min(reach - counts[i], max(1, left * weights[i] // mass), surplus)
            counts[i] = counts[i] + more
            surplus = surplus - more
    return np.array(counts)


def bell_draw(key, shape, width, most, split=(), dtype=jnp.bfloat16):
    values = jax.random.normal(key, shape, jnp.float32) * width
    if len(split) > 0:
        values = steps_of(key, shape, split, -0.22, 0.18) * values
    return jnp.clip(values, min=-most, max=most).astype(dtype)


def setup_inputs(seed: int = 0) -> dict:
    splits = jax.random.split(jax.random.key(seed), 13)
    feats = bell_draw(splits[0], (NODES, F), 1.0, 6.0, ((0, 32),))
    weight = bell_draw(splits[1], (F, F), F ** -0.5, 0.375)
    cotangent = bell_draw(splits[2], (NODES, F), 1.0, 6.0, ((0, 32),))
    labels = plant(jax.random.randint(splits[3], (NODES,), -86, 172), jax.random.fold_in(splits[3], 1), -86, 171).astype(jnp.int32)
    tile_vals = bell_draw(splits[4], (N_GRP, N_BLK, N_BLK, TPB, TILE, TILE), (N_BLK * TPB * TILE // RT) ** -0.5, 0.09375, ((0, 4), (1, 8)))
    tile_row = plant(jax.random.randint(splits[5], (N_GRP, N_BLK, N_BLK, TPB), 0, RT), jax.random.fold_in(splits[5], 1), 0, RT - 1).astype(jnp.int32)
    tile_col = plant(jax.random.randint(splits[6], (N_GRP, N_BLK, N_BLK, TPB), 0, RT), jax.random.fold_in(splits[6], 1), 0, RT - 1).astype(jnp.int32)
    tile_count = draw_tile_count(jax.random.fold_in(splits[12], 71), 0)
    hub_vals = bell_draw(splits[8], (N_GRP, N_BLK, HUB, TILE, TILE), (N_BLK * TPB * TILE // RT) ** -0.5, 0.09375, ((0, 4), (1, 8)))
    hub_col = plant(jax.random.randint(splits[9], (N_GRP, N_BLK, HUB), 0, RT), jax.random.fold_in(splits[9], 1), 0, RT - 1).astype(jnp.int32)
    hub_dest_keys = jax.random.split(jax.random.fold_in(splits[10], 1), N_GRP * N_BLK * HUB // HUB)
    hub_dest_turns = jax.random.permutation(jax.random.fold_in(splits[10], 3), N_GRP * N_BLK * HUB // HUB)
    hub_dest = jax.vmap(lambda own, number: assign_block(jax.random.fold_in(splits[10], 2), own, number, HUB, N_GRP, 1, CAP, 2))(hub_dest_keys, hub_dest_turns).reshape((N_GRP, N_BLK, HUB, 1))
    hub_row = plant(jax.random.randint(splits[11], (N_GRP, N_BLK, HUB), 0, RT), jax.random.fold_in(splits[11], 1), 0, RT - 1).astype(jnp.int32)
    return {"feats": feats, "weight": weight, "cotangent": cotangent, "labels": labels, "tile_vals": tile_vals, "tile_row": tile_row, "tile_col": tile_col, "tile_count": tile_count, "hub_vals": hub_vals, "hub_col": hub_col, "hub_dest": hub_dest, "hub_row": hub_row}


def forward_device(inputs):
    dev_vals, dev_rows, dev_cols, dev_count, panels = inputs
    picked = panels[jnp.arange(N_BLK)[:, None], dev_cols]
    product = jnp.einsum('ctij,ctjf->ctif', dev_vals.astype(jnp.float32), picked.astype(jnp.float32))
    live_mask = (jnp.arange(TPB)[None, :] < dev_count[:, None]).astype(jnp.float32)
    placing = (dev_rows[..., None] == jnp.arange(RT)[None, None, :]).astype(jnp.float32) * live_mask[..., None]
    return jnp.einsum('ctr,ctif->rif', placing, product)

def backward_group(inputs):
    grp_vals, grp_rows, grp_cols, grp_count, grp_grad = inputs

    def add_block(carry, xs):
        dev_vals, dev_rows, dev_cols, dev_count, grad_tiles = xs
        picked = grad_tiles[dev_rows]
        product = jnp.einsum('ctij,ctif->ctjf', dev_vals.astype(jnp.float32), picked.astype(jnp.float32))
        live_mask = (jnp.arange(TPB)[None, :] < dev_count[:, None]).astype(jnp.float32)
        placing = (dev_cols[..., None] == jnp.arange(RT)[None, None, :]).astype(jnp.float32) * live_mask[..., None]
        return (carry + jnp.einsum('ctr,ctjf->crjf', placing, product), None)
    start_acc = jnp.zeros((N_BLK, RT, TILE, F), jnp.float32)
    result, _ = lax.scan(add_block, start_acc, (grp_vals, grp_rows, grp_cols, grp_count, grp_grad))
    return result

def reference(feats, weight, cotangent, labels, tile_vals, tile_row, tile_col, tile_count, hub_vals, hub_col, hub_dest, hub_row):
    proj = jnp.dot(feats, weight, preferred_element_type=jnp.float32).astype(jnp.bfloat16)
    proj_tiles = proj.reshape(N_GRP, N_BLK, RT, TILE, F)
    group_of = jnp.repeat(jnp.arange(N_GRP), N_BLK)
    panels_all = proj_tiles[group_of]
    agg = lax.map(forward_device, (tile_vals.reshape(N_GRP * N_BLK, N_BLK, TPB, TILE, TILE), tile_row.reshape(N_GRP * N_BLK, N_BLK, TPB), tile_col.reshape(N_GRP * N_BLK, N_BLK, TPB), tile_count.reshape(N_GRP * N_BLK, N_BLK), panels_all))
    agg = agg.reshape(N_GRP, N_BLK, RT, TILE, F)
    grp_index = jnp.arange(N_GRP)[:, None, None]
    blk_index = jnp.arange(N_BLK)[None, :, None]
    dest = hub_dest[..., 0]
    hub_src = proj_tiles[grp_index, blk_index, hub_col]
    hub_part = jnp.einsum('gbhij,gbhjf->gbhif', hub_vals.astype(jnp.float32), hub_src.astype(jnp.float32))
    agg = agg.at[dest, blk_index, hub_row].add(hub_part)
    agg_rows = agg.reshape(NODES, F)
    layer_out = jax.nn.silu(agg_rows).astype(jnp.bfloat16)
    sigmoid_z = jax.nn.sigmoid(agg_rows)
    slope = sigmoid_z * (1.0 + agg_rows * (1.0 - sigmoid_z))
    keep = (labels >= 0).astype(jnp.float32)[:, None]
    grad_agg = (cotangent.astype(jnp.float32) * keep * slope).astype(jnp.bfloat16)
    grad_tiles = grad_agg.reshape(N_GRP, N_BLK, RT, TILE, F)
    grad_proj = lax.map(backward_group, (tile_vals, tile_row, tile_col, tile_count, grad_tiles))
    hub_grad = grad_tiles[dest, blk_index, hub_row]
    hub_back = jnp.einsum('gbhij,gbhif->gbhjf', hub_vals.astype(jnp.float32), hub_grad.astype(jnp.float32))
    grad_proj = grad_proj.at[grp_index, blk_index, hub_col].add(hub_back)
    grad_rows = grad_proj.reshape(NODES, F).astype(jnp.bfloat16)
    grad_weight = jnp.dot(feats.T, grad_rows, preferred_element_type=jnp.float32) * (1.0 / math.sqrt(NODES))
    grad_feats = jnp.dot(grad_rows, weight.T, preferred_element_type=jnp.float32).astype(jnp.bfloat16)
    return (layer_out, grad_feats, grad_weight)
```

```python
import functools
import math

import jax
import jax.numpy as jnp
from jax import lax
from jax.experimental import pallas as pl
from jax.experimental.pallas import tpu as pltpu
from jax.sharding import PartitionSpec as P

F32 = jnp.float32
BF16 = jnp.bfloat16
UNROLL = 16
SMEM = pl.BlockSpec(memory_space=pltpu.SMEM)
VMEM = pl.BlockSpec(memory_space=pltpu.VMEM)
ANY = pl.BlockSpec(memory_space=pl.ANY)


def dot(a, b, dims):
    return lax.dot_general(a, b, (dims, ((), ())), preferred_element_type=F32)


def call(kernel, name, out_shape, in_specs, out_specs, scratch, flops, moved):
    return pl.pallas_call(
        kernel,
        out_shape=out_shape,
        in_specs=in_specs,
        out_specs=out_specs,
        scratch_shapes=scratch,
        compiler_params=pltpu.CompilerParams(vmem_limit_bytes=40 << 20),
        cost_estimate=pl.CostEstimate(flops=flops, bytes_accessed=moved, transcendentals=0),
        name=name,
    )


def fetch_pair(ids, vals, buf, sem):
    slots = vals.shape[1]
    copies = [
        pltpu.make_async_copy(vals.at[ids[k]], buf.at[pl.ds(k * slots, slots)], sem.at[k])
        for k in range(2)
    ]
    for copy in copies:
        copy.start()
    return copies


def pair_loop(ids, cnt, picks, places, buf, source, total, spread):
    slots = buf.shape[0] // 2
    row_tiles = source.shape[0] if spread == "places" else source.shape[0] // 2
    trash = total.shape[0] - 1
    first, second = cnt[ids[0]], cnt[ids[1]]
    used = first + second
    contract = ((1,), (0,)) if spread == "picks" else ((0,), (0,))

    def body(step, carry):
        products = []
        for u in range(UNROLL):
            at = step * UNROLL + u
            late = at >= first
            live = at < used
            slot = jnp.where(live, jnp.where(late, at - first, at), 0)
            block = jnp.where(late, ids[1], ids[0])
            shift = jnp.where(late, 1, 0)
            pick = picks[block, slot]
            place = places[block, slot]
            if spread == "picks":
                pick = pick + shift * row_tiles
            else:
                place = place + shift * row_tiles
            place = jnp.where(live, place, trash)
            tile = buf[shift * slots + slot]
            products.append((place, dot(tile, source[pick], contract)))
        for place, product in products:
            total[place] += product
        return carry

    lax.fori_loop(0, (used + UNROLL - 1) // UNROLL, body, 0)


def forward_pair(has_acc, ids, cnt, rows, cols, *refs):
    if has_acc:
        acc, block_a, block_b, weight, vals, out, buf, panel, total, sem = refs
    else:
        block_a, block_b, weight, vals, out, buf, panel, total, sem = refs
    copies = fetch_pair(ids, vals, buf, sem)
    row_tiles, size, width = out.shape
    for k, block in enumerate((block_a, block_b)):
        proj = dot(block[...], weight[...], ((1,), (0,))).astype(BF16)
        panel[pl.ds(k * row_tiles, row_tiles)] = proj.reshape(row_tiles, size, width)
    if has_acc:
        total[pl.ds(0, row_tiles)] = acc[...]
    else:
        total[...] = jnp.zeros_like(total)
    for copy in copies:
        copy.wait()
    pair_loop(ids, cnt, cols, rows, buf, panel, total, "picks")
    out[...] = total[pl.ds(0, row_tiles)]


def hub_products(me, dest, cols, feats, weight, tiles, send, panel, tally):
    groups = send.shape[0]
    cap = send.shape[1]
    row_tiles, size, width = panel.shape
    proj = dot(feats[...], weight[...], ((1,), (0,))).astype(BF16)
    panel[...] = proj.reshape(row_tiles, size, width)
    for k in range(groups):
        tally[k] = 0
    for h in range(tiles.shape[0]):
        to = dest[me[0], h] ^ me[0]
        rank = jnp.minimum(tally[to], cap - 1)
        tally[to] = rank + 1
        product = dot(tiles[h], panel[cols[h]], ((1,), (0,)))
        send[to, rank] = product.astype(BF16)


def each_hub(me, dest, groups, count, cap, visit):
    for k in range(groups):
        source = me[0] ^ k

        def body(h, rank, k=k, source=source):
            mine = dest[source, h] == me[0]

            @pl.when(mine)
            def _():
                visit(k, source, h, jnp.minimum(rank, cap - 1))

            return rank + mine.astype(jnp.int32)

        lax.fori_loop(0, count, body, jnp.int32(0))


def hub_add(groups, me, dest, hub_rows, *refs):
    acc, parts, out = refs[0], refs[1:-1], refs[-1]
    out[...] = acc[...]

    def visit(k, source, h, rank):
        out[hub_rows[source, h]] += parts[k][rank].astype(F32)

    each_hub(me, dest, groups, dest.shape[1], parts[0].shape[0], visit)


def last_forward(
    ids, cnt, rows, cols, me, dest, hub_rows, acc, block_a, block_b, weight, vals, cot,
    layer_out, grad, back, buf, panel, total, sem,
):
    copies = fetch_pair(ids, vals, buf, sem)
    row_tiles, size, width = grad.shape
    for k, block in enumerate((block_a, block_b)):
        proj = dot(block[...], weight[...], ((1,), (0,))).astype(BF16)
        panel[pl.ds(k * row_tiles, row_tiles)] = proj.reshape(row_tiles, size, width)
    total[pl.ds(0, row_tiles)] = acc[...]
    for copy in copies:
        copy.wait()
    pair_loop(ids, cnt, cols, rows, buf, panel, total, "picks")

    def finish(r, carry):
        agg = total[r]
        sig = jax.nn.sigmoid(agg)
        layer_out[r] = (agg * sig).astype(BF16)
        slope = sig * (1.0 + agg * (1.0 - sig))
        grad[r] = (cot[r].astype(F32) * slope).astype(BF16)
        return carry

    lax.fori_loop(0, row_tiles, finish, 0)

    def visit(k, source, h, rank):
        back[k, rank] = grad[hub_rows[source, h]]

    each_hub(me, dest, back.shape[0], dest.shape[1], back.shape[1], visit)


def backward_pair(has_gw, ids, cnt, rows, cols, *refs):
    if has_gw:
        gw, grad, block_a, block_b, vals, part_a, part_b, gw_out, buf, total, sem = refs
    else:
        grad, block_a, block_b, vals, part_a, part_b, gw_out, buf, total, sem = refs
    copies = fetch_pair(ids, vals, buf, sem)
    row_tiles, size, width = grad.shape
    total[...] = jnp.zeros_like(total)
    for copy in copies:
        copy.wait()
    pair_loop(ids, cnt, rows, cols, buf, grad, total, "places")
    part_a[...] = total[pl.ds(0, row_tiles)].astype(BF16)
    part_b[...] = total[pl.ds(row_tiles, row_tiles)]
    sums = gw[...] if has_gw else jnp.zeros(gw_out.shape, F32)
    for k, block in enumerate((block_a, block_b)):
        mine = total[pl.ds(k * row_tiles, row_tiles)].astype(BF16).reshape(row_tiles * size, width)
        sums += dot(block[...], mine, ((0,), (0,)))
    gw_out[...] = sums


def hub_backward(groups, me, dest, cols, gw, own, feats, tiles, *refs):
    parts, (out, gw_out, slots, total, tally) = refs[:groups], refs[groups:]
    row_tiles, size, width = out.shape
    cap = parts[0].shape[0]
    for k in range(groups):
        slots[pl.ds(k * cap, cap)] = parts[k][...]
        tally[k] = 0
    total[...] = jnp.zeros_like(total)
    products = []
    for h in range(tiles.shape[0]):
        source = dest[me[0], h] ^ me[0]
        rank = jnp.minimum(tally[source], cap - 1)
        tally[source] = rank + 1
        products.append(dot(tiles[h], slots[source * cap + rank], ((0,), (0,))))
        if len(products) == 8 or h == tiles.shape[0] - 1:
            for back, product in enumerate(products):
                total[cols[h + 1 - len(products) + back]] += product
            products = []
    out[...] = own[...] + total[...]
    mine = total[...].astype(BF16).reshape(row_tiles * size, width)
    gw_out[...] = gw[...] + dot(feats[...], mine, ((0,), (0,)))


def last_backward(count, *refs):
    own, parts, weight, out = refs[0], refs[1 : 1 + count], refs[-2], refs[-1]
    sums = own[...]
    for part in parts:
        sums = sums + part[...].astype(F32)
    out[...] = dot(sums.astype(BF16).reshape(out.shape), weight[...], ((1,), (1,))).astype(BF16)


def tree_sum(values):
    while len(values) > 1:
        values = [a + b for a, b in zip(values[::2], values[1::2])]
    return values[0]


def local(
    feats,
    weight,
    cotangent,
    labels,
    tile_vals,
    tile_row,
    tile_col,
    tile_count,
    hub_vals,
    hub_col,
    hub_dest,
    hub_row,
):
    n_blocks = lax.axis_size("blk")
    n_groups = lax.axis_size("grp")
    n_chips = n_blocks // 2
    my_block = lax.axis_index("blk").astype(jnp.int32)
    my_group = lax.axis_index("grp").astype(jnp.int32)
    core = my_block % 2
    rows_dev, width = feats.shape
    size = tile_vals.shape[-1]
    row_tiles = rows_dev // size
    slots = tile_vals.shape[3]
    hubs = hub_vals.shape[2]
    cap = max(2, hubs // 4)
    vals = tile_vals[0, 0]
    rows, cols, cnt = tile_row[0, 0], tile_col[0, 0], tile_count[0, 0]
    dest, hub_rows = hub_dest[:, 0, :, 0], hub_row[:, 0, :]
    hub_tiles, hub_cols = hub_vals[0, 0], hub_col[0, 0]
    me = my_group.reshape(1)
    panel = (row_tiles, size, width)
    relay = n_chips == 4

    def swap(value):
        return lax.ppermute(value, "blk", [(i, i ^ 1) for i in range(n_blocks)])

    def across(value, mask, chips=None):
        chosen = range(n_chips) if chips is None else chips
        pairs = [(2 * c + k, 2 * (c ^ mask) + k) for c in chosen for k in range(2)]
        return lax.ppermute(value, "blk", pairs)

    def group(value, mask):
        return lax.ppermute(value, "grp", [(i, i ^ mask) for i in range(n_groups)])

    def ids_of(mask):
        chip = (my_block // 2) ^ mask
        return jnp.stack([2 * chip + 1 - core, 2 * chip + core])

    moved = 4 << 20
    tile_flops = 2 * size * size * width
    pair_flops = 2 * slots * tile_flops
    buf = pltpu.VMEM((2 * slots, size, size), BF16)
    sems = pltpu.SemaphoreType.DMA((2,))
    acc_shape = jax.ShapeDtypeStruct(panel, F32)

    got = {0: feats}
    if relay:
        got[2] = across(feats, 2)
        got[1] = across(feats, 1)
        direct = across(feats, 3, (1, 2))
        passed = across(got[2], 1, (1, 2))
        got[3] = direct + passed
    else:
        for mask in range(1, n_chips):
            got[mask] = across(feats, mask)
    pairs = {mask: swap(value) for mask, value in got.items()}

    send = call(
        hub_products,
        "hub_products",
        jax.ShapeDtypeStruct((n_groups, cap, size, width), BF16),
        [SMEM, SMEM, SMEM, VMEM, VMEM, VMEM],
        VMEM,
        [pltpu.VMEM(panel, BF16), pltpu.SMEM((n_groups,), jnp.int32)],
        hubs * tile_flops,
        moved,
    )(me, dest, hub_cols, feats, weight, hub_tiles)
    hub_parts = [send[0]] + [group(send[k], k) for k in range(1, n_groups)]

    order = [m for m in range(n_chips) if m != n_chips - 1]
    last = n_chips - 1

    acc = None
    for mask in order:
        acc = call(
            functools.partial(forward_pair, acc is not None),
            "forward_pair",
            acc_shape,
            [SMEM] * 4 + [VMEM] * (3 if acc is None else 4) + [ANY],
            VMEM,
            [
                buf,
                pltpu.VMEM((2 * row_tiles, size, width), BF16),
                pltpu.VMEM((row_tiles + 1, size, width), F32),
                sems,
            ],
            pair_flops,
            moved,
        )(
            ids_of(mask), cnt, rows, cols, *(() if acc is None else (acc,)),
            pairs[mask], got[mask], weight, vals,
        )
        if mask == order[1]:
            acc = call(
                functools.partial(hub_add, n_groups),
                "hub_add",
                acc_shape,
                [SMEM] * 3 + [VMEM] * (1 + n_groups),
                VMEM,
                [],
                1 << 20,
                moved,
            )(me, dest, hub_rows, acc, *hub_parts)

    cot = jnp.where(labels[:, None] >= 0, cotangent, jnp.zeros_like(cotangent)).reshape(panel)
    layer_out, grad, back = call(
        last_forward,
        "last_forward",
        (
            jax.ShapeDtypeStruct(panel, BF16),
            jax.ShapeDtypeStruct(panel, BF16),
            jax.ShapeDtypeStruct((n_groups, cap, size, width), BF16),
        ),
        [SMEM] * 7 + [VMEM] * 4 + [ANY, VMEM],
        (VMEM, VMEM, VMEM),
        [
            buf,
            pltpu.VMEM((2 * row_tiles, size, width), BF16),
            pltpu.VMEM((row_tiles + 1, size, width), F32),
            sems,
        ],
        pair_flops,
        moved,
    )(
        ids_of(last), cnt, rows, cols, me, dest, hub_rows, acc,
        pairs[last], got[last], weight, vals, cot,
    )

    back_parts = [back[0]] + [group(back[k], k) for k in range(1, n_groups)]

    gw = None
    arrived = []
    from_ends = None
    for mask in reversed(range(n_chips)):
        part_other, part_own, gw = call(
            functools.partial(backward_pair, gw is not None),
            "backward_pair",
            (
                jax.ShapeDtypeStruct(panel, BF16),
                acc_shape,
                jax.ShapeDtypeStruct((width, width), F32),
            ),
            [SMEM] * 4 + [VMEM] * (3 if gw is None else 4) + [ANY],
            (VMEM, VMEM, VMEM),
            [buf, pltpu.VMEM((2 * row_tiles + 1, size, width), F32), sems],
            pair_flops,
            moved,
        )(
            ids_of(mask), cnt, rows, cols, *(() if gw is None else (gw,)),
            grad, pairs[mask], got[mask], vals,
        )
        theirs = swap(part_other)
        if mask == 0:
            arrived.append(theirs)
            break
        both = part_own + theirs.astype(F32)
        if relay and mask == 3:
            both = both.astype(BF16)
            from_ends = across(both, 1, (0, 3))
            arrived.append(across(both, 3, (1, 2)))
        else:
            if relay and mask == 2:
                both = both + from_ends.astype(F32)
            arrived.append(across(both.astype(BF16), mask))

    own_sum, gw = call(
        functools.partial(hub_backward, n_groups),
        "hub_backward",
        (acc_shape, jax.ShapeDtypeStruct((width, width), F32)),
        [SMEM] * 3 + [VMEM] * (4 + n_groups),
        (VMEM, VMEM),
        [
            pltpu.VMEM((n_groups * cap, size, width), BF16),
            pltpu.VMEM(panel, F32),
            pltpu.SMEM((n_groups,), jnp.int32),
        ],
        hubs * tile_flops,
        moved,
    )(me, dest, hub_cols, gw, part_own, feats, hub_tiles, *back_parts)

    half = width // 2
    halves = gw.reshape(2, half, width).astype(BF16)
    kept = lax.dynamic_index_in_dim(halves, core, 0, keepdims=False)
    given = lax.dynamic_index_in_dim(halves, 1 - core, 0, keepdims=False)
    share = (kept.astype(F32) + swap(given).astype(F32)).astype(BF16)
    terms = [share] + [group(share, k) for k in range(1, n_groups)]
    share = tree_sum([t.astype(F32) for t in terms]).astype(BF16)
    terms = [share] + [across(share, m) for m in range(1, n_chips)]
    share = tree_sum([t.astype(F32) for t in terms]) * (1.0 / math.sqrt(rows_dev * n_blocks * n_groups))
    other = swap(share)
    grad_weight = jnp.concatenate(
        [jnp.where(core == 0, share, other), jnp.where(core == 0, other, share)], axis=0
    )

    grad_feats = call(
        functools.partial(last_backward, len(arrived)),
        "last_backward",
        jax.ShapeDtypeStruct((rows_dev, width), BF16),
        [VMEM] * (2 + len(arrived)),
        VMEM,
        [],
        2 * rows_dev * width * width,
        moved,
    )(own_sum, *arrived, weight)
    return (layer_out.reshape(rows_dev, width), grad_feats, grad_weight)


def solution(mesh):
    in_specs = (
        P(("grp", "blk"), None),
        P(),
        P(("grp", "blk"), None),
        P(("grp", "blk")),
        P("grp", "blk", None, None, None, None),
        P("grp", "blk", None, None),
        P("grp", "blk", None, None),
        P("grp", "blk", None),
        P("grp", "blk", None, None, None),
        P("grp", "blk", None),
        P(None, "blk", None, None),
        P(None, "blk", None),
    )
    out_specs = (P(("grp", "blk"), None), P(("grp", "blk"), None), P())
    return jax.shard_map(local, mesh=mesh, in_specs=in_specs, out_specs=out_specs, check_vma=False)
```

```python
import functools
import math

import jax
import jax.numpy as jnp
from jax import lax
from jax.experimental import pallas as pl
from jax.experimental.pallas import tpu as pltpu
from jax.sharding import PartitionSpec as P

F32 = jnp.float32
BF16 = jnp.bfloat16
UNROLL = 16
SMEM = pl.BlockSpec(memory_space=pltpu.SMEM)
VMEM = pl.BlockSpec(memory_space=pltpu.VMEM)
HBM = pl.BlockSpec(memory_space=pltpu.HBM)


def dot(a, b, dims):
    return lax.dot_general(a, b, (dims, ((), ())), preferred_element_type=F32)


def call(kernel, name, out_shape, in_specs, out_specs, scratch, flops, moved, vmem=14):
    return pl.pallas_call(
        kernel,
        out_shape=out_shape,
        in_specs=in_specs,
        out_specs=out_specs,
        scratch_shapes=scratch,
        compiler_params=pltpu.CompilerParams(vmem_limit_bytes=vmem << 20),
        cost_estimate=pl.CostEstimate(flops=flops, bytes_accessed=moved, transcendentals=0),
        name=name,
    )


class Meta:
    def __init__(self, blocks, slots):
        self.slots = slots
        starts = [0]
        for size in (3, blocks, blocks * slots, blocks * slots):
            starts.append(starts[-1] + size)
        self.at = starts

    def block(self, ref, mask, other):
        chip = ref[1] ^ mask
        return 2 * chip + (ref[2] ^ 1 if other else ref[2])

    def count(self, ref, block):
        return ref[self.at[1] + block]

    def row(self, ref, block, slot):
        return ref[self.at[2] + block * self.slots + slot]

    def col(self, ref, block, slot):
        return ref[self.at[3] + block * self.slots + slot]


def stage_tiles(meta, pos, vals, *refs):
    outs, sem = refs[:-1], refs[-1]
    copies = []
    for mask, out in enumerate(outs):
        for k, side in enumerate((1, 0)):
            block = vals.at[meta.block(pos, mask, side)]
            copies.append(pltpu.make_async_copy(block, out.at[k], sem.at[2 * mask + k]))
    for copy in copies:
        copy.start()
    for copy in copies:
        copy.wait()


def tile_loop(meta, ints, mask, sides, forward, tiles, sources, total):
    blocks = [meta.block(ints, mask, side) for side in sides]
    trash = total.shape[0] - 1
    row_tiles = trash // (1 if forward else len(blocks))
    first = meta.count(ints, blocks[0])
    used = first if len(blocks) == 1 else first + meta.count(ints, blocks[1])
    contract = ((1,), (0,)) if forward else ((0,), (0,))

    def body(step, carry):
        products = []
        for u in range(UNROLL):
            at = step * UNROLL + u
            live = at < used
            if len(blocks) == 1:
                block, late, shift, slot = blocks[0], 1 - sides[0], 0, jnp.where(live, at, 0)
            else:
                late = jnp.where(at >= first, 1, 0)
                block = jnp.where(late == 1, blocks[1], blocks[0])
                shift = late * row_tiles
                slot = jnp.where(live, at - late * first, 0)
            row, col = meta.row(ints, block, slot), meta.col(ints, block, slot)
            pick, place = (col + shift, row) if forward else (row, col + shift)
            place = jnp.where(live, place, trash)
            products.append((place, dot(tiles[late, slot], sources[pick], contract)))
        for place, product in products:
            total[place] += product
        return carry

    lax.fori_loop(0, (used + UNROLL - 1) // UNROLL, body, 0)


def gather_panels(parts, panel):
    start = 0
    for part in parts:
        panel[pl.ds(start, part.shape[0])] = part[...]
        start += part.shape[0]


def forward_blocks(meta, mask, sides, has_acc, ints, *refs):
    acc, refs = (refs[0], refs[1:]) if has_acc else (None, refs)
    feats, (tiles, out, panel, total) = refs[:-4], refs[-4:]
    row_tiles = out.shape[0]
    gather_panels(feats, panel)
    if has_acc:
        total[pl.ds(0, row_tiles)] = acc[...]
    else:
        total[...] = jnp.zeros_like(total)
    tile_loop(meta, ints, mask, sides, True, tiles, panel, total)
    out[...] = total[pl.ds(0, row_tiles)]


def hub_products(groups, pos, dest, cols, feats, tiles, send, tally):
    cap = send.shape[1]
    me = pos[0]
    for k in range(groups):
        tally[k] = 0
    for h in range(tiles.shape[0]):
        to = dest[me, h] ^ me
        rank = jnp.minimum(tally[to], cap - 1)
        tally[to] = rank + 1
        send[to, rank] = dot(tiles[h], feats[cols[h]], ((1,), (0,))).astype(BF16)


def each_hub(pos, dest, groups, cap, visit):
    me = pos[0]
    for k in range(groups):
        source = me ^ k

        def body(h, rank, k=k, source=source):
            mine = dest[source, h] == me

            @pl.when(mine)
            def _():
                visit(k, source, h, jnp.minimum(rank, cap - 1))

            return rank + mine.astype(jnp.int32)

        lax.fori_loop(0, dest.shape[1], body, jnp.int32(0))


def hub_add(pos, dest, rows, *refs):
    acc, parts, out = refs[0], refs[1:-1], refs[-1]
    out[...] = acc[...]

    def visit(k, source, h, rank):
        out[rows[source, h]] += parts[k][rank].astype(F32)

    each_hub(pos, dest, len(parts), parts[0].shape[0], visit)


def last_forward(meta, mask, ints, dest, rows, acc, *refs):
    feats, refs = refs[:-9], refs[-9:]
    weight, tiles, cot, layer_out, grad, back, gw, panel, total = refs
    row_tiles = grad.shape[0]
    gather_panels(feats, panel)
    total[pl.ds(0, row_tiles)] = acc[...]
    tile_loop(meta, ints, mask, (1,), True, tiles, panel, total)
    sums = jnp.zeros(gw.shape, F32)
    for r in range(row_tiles):
        neighbours = total[r].astype(BF16)
        agg = dot(neighbours, weight[...], ((1,), (0,)))
        sig = jax.nn.sigmoid(agg)
        layer_out[r] = (agg * sig).astype(BF16)
        slope = sig * (1.0 + agg * (1.0 - sig))
        grad[r] = (cot[r].astype(F32) * slope).astype(BF16)
        sums += dot(neighbours, grad[r], ((0,), (0,)))
    gw[...] = sums

    def visit(k, source, h, rank):
        back[k, rank] = grad[rows[source, h]]

    each_hub(ints, dest, back.shape[0], back.shape[1], visit)


def backward_blocks(meta, mask, sides, ints, grad, tiles, *refs):
    parts, total = refs[:-1], refs[-1]
    row_tiles = grad.shape[0]
    total[...] = jnp.zeros_like(total)
    tile_loop(meta, ints, mask, sides, False, tiles, grad, total)
    for k, part in enumerate(parts):
        part[...] = total[pl.ds(k * row_tiles, row_tiles)].astype(part.dtype)


def last_products(groups, meta, ints, dest, cols, grad, tiles, hub_tiles, *refs):
    parts, (other, out, total, slots, tally) = refs[:groups], refs[groups:]
    row_tiles, cap = out.shape[0], parts[0].shape[0]
    me = ints[0]
    total[...] = jnp.zeros_like(total)
    tile_loop(meta, ints, 0, (1, 0), False, tiles, grad, total)
    other[...] = total[pl.ds(0, row_tiles)].astype(BF16)
    for k in range(groups):
        slots[pl.ds(k * cap, cap)] = parts[k][...]
        tally[k] = 0
    products = []
    for h in range(hub_tiles.shape[0]):
        source = dest[me, h] ^ me
        rank = jnp.minimum(tally[source], cap - 1)
        tally[source] = rank + 1
        products.append((cols[h], dot(hub_tiles[h], slots[source * cap + rank], ((0,), (0,)))))
        if len(products) == 8 or h == hub_tiles.shape[0] - 1:
            for place, product in products:
                total[row_tiles + place] += product
            products = []
    out[...] = total[pl.ds(row_tiles, row_tiles)]


def last_backward(count, *refs):
    own, parts, weight, out = refs[0], refs[1 : 1 + count], refs[-2], refs[-1]
    sums = own[...]
    for part in parts:
        sums = sums + part[pl.ds(0, own.shape[0])].astype(F32)
    out[...] = dot(sums.astype(BF16).reshape(out.shape), weight[...], ((1,), (1,))).astype(BF16)


def after(value, *others):
    return lax.optimization_barrier((value, *others))[0]


def tree_sum(values):
    while len(values) > 1:
        values = [a + b for a, b in zip(values[::2], values[1::2])]
    return values[0]


def local(
    feats,
    weight,
    cotangent,
    labels,
    tile_vals,
    tile_row,
    tile_col,
    tile_count,
    hub_vals,
    hub_col,
    hub_dest,
    hub_row,
):
    n_blocks = lax.axis_size("blk")
    n_groups = lax.axis_size("grp")
    n_chips = n_blocks // 2
    my_block = lax.axis_index("blk").astype(jnp.int32)
    my_group = lax.axis_index("grp").astype(jnp.int32)
    core = my_block % 2
    rows_dev, width = feats.shape
    size = tile_vals.shape[-1]
    row_tiles = rows_dev // size
    slots = tile_vals.shape[3]
    hubs = hub_vals.shape[2]
    cap = max(2, hubs // 4)
    vals = tile_vals[0, 0]
    hub_tiles = hub_vals[0, 0]
    panel = (row_tiles, size, width)
    relay = n_chips == 4
    meta = Meta(n_blocks, slots)
    pos = jnp.stack([my_group, my_block // 2, core])
    ints = jnp.concatenate([pos] + [v.reshape(-1) for v in (tile_count, tile_row, tile_col)])
    dest, hub_rows, hub_cols = hub_dest[:, 0, :, 0], hub_row[:, 0, :], hub_col[0, 0]

    def swap(value):
        return lax.ppermute(value, "blk", [(i, i ^ 1) for i in range(n_blocks)])

    def across(value, mask, chips=None):
        chosen = range(n_chips) if chips is None else chips
        pairs = [(2 * c + k, 2 * (c ^ mask) + k) for c in chosen for k in range(2)]
        return lax.ppermute(value, "blk", pairs)

    def group(value, mask):
        return lax.ppermute(value, "grp", [(i, i ^ mask) for i in range(n_groups)])

    moved, tile_flops = 100 * (4 << 20), 100 * 2 * size * size * width
    block_flops = slots * tile_flops
    acc_shape = jax.ShapeDtypeStruct(panel, F32)
    tiles = call(
        functools.partial(stage_tiles, meta),
        "stage_tiles",
        (jax.ShapeDtypeStruct((2, slots, size, size), BF16),) * n_chips,
        [SMEM, HBM],
        (VMEM,) * n_chips,
        [pltpu.SemaphoreType.DMA((n_blocks,))],
        1,
        moved,
        48,
    )(pos, vals)

    def forward(mask, sides, acc, blocks):
        return call(
            functools.partial(forward_blocks, meta, mask, sides, acc is not None),
            "forward_blocks",
            acc_shape,
            [SMEM] + [VMEM] * (len(blocks) + (1 if acc is None else 2)),
            VMEM,
            [
                pltpu.VMEM((len(sides) * row_tiles, size, width), BF16),
                pltpu.VMEM((row_tiles + 1, size, width), F32),
            ],
            len(sides) * block_flops,
            moved,
        )(ints, *(() if acc is None else (acc,)), *blocks, tiles[mask])

    def backward(mask, sides, grad):
        return call(
            functools.partial(backward_blocks, meta, mask, sides),
            "backward_blocks",
            tuple(jax.ShapeDtypeStruct(panel, BF16 if side else F32) for side in sides),
            [SMEM, VMEM, VMEM],
            (VMEM,) * len(sides),
            [
                pltpu.VMEM((len(sides) * row_tiles + 1, size, width), F32),
            ],
            len(sides) * block_flops,
            moved,
        )(ints, grad, tiles[mask])

    last = n_chips - 1
    feats = feats.reshape(panel)
    got, pairs = {0: [feats]}, {0: [swap(feats)]}
    if relay:
        got[2] = [across(feats, 2)]
        got[1] = [across(feats, 1)]
    else:
        for mask in range(1, n_chips):
            got[mask] = [across(feats, mask)]

    send = call(
        functools.partial(hub_products, n_groups),
        "hub_products",
        jax.ShapeDtypeStruct((n_groups, cap, size, width), BF16),
        [SMEM, SMEM, SMEM, VMEM, VMEM],
        VMEM,
        [pltpu.SMEM((n_groups,), jnp.int32)],
        hubs * tile_flops,
        moved,
    )(pos, dest, hub_cols, after(feats, *pairs[0]), hub_tiles)
    hub_parts = [send[0]] + [group(send[k], k) for k in range(1, n_groups)]
    acc = forward(0, (1, 0), None, (*pairs[0], *got[0]))
    if relay:
        passed = across(after(got[2][0], acc), 1, (1, 2))
        direct = across(after(feats, acc, got[2][0]), 3, (1, 2))
    acc = call(
        hub_add,
        "hub_add",
        acc_shape,
        [SMEM] * 3 + [VMEM] * (1 + n_groups),
        VMEM,
        [],
        1 << 20,
        moved,
    )(pos, dest, hub_rows, acc, *hub_parts)
    for mask in range(1, last):
        pairs[mask] = [swap(part) for part in got[mask]]
        acc = forward(mask, (1, 0), acc, (*pairs[mask], *got[mask]))
    if relay:
        got[last] = [after(passed, acc) + direct]
    pairs[last] = [swap(part) for part in got[last]]
    acc = forward(last, (0,), acc, got[last])

    cot = jnp.where(labels[:, None] >= 0, cotangent, jnp.zeros_like(cotangent)).reshape(panel)
    layer_out, grad, back, gw = call(
        functools.partial(last_forward, meta, last),
        "last_forward",
        (
            jax.ShapeDtypeStruct(panel, BF16),
            jax.ShapeDtypeStruct(panel, BF16),
            jax.ShapeDtypeStruct((n_groups, cap, size, width), BF16),
            jax.ShapeDtypeStruct((width, width), F32),
        ),
        [SMEM] * 3 + [VMEM] * (4 + len(pairs[last])),
        (VMEM,) * 4,
        [
            pltpu.VMEM(panel, BF16),
            pltpu.VMEM((row_tiles + 1, size, width), F32),
        ],
        block_flops,
        moved,
    )(ints, dest, hub_rows, acc, *pairs[last], weight, tiles[last], cot)

    (part_other,) = backward(last, (1,), grad)
    theirs = swap(part_other)
    (part_own,) = backward(last, (0,), grad)
    both = (part_own + theirs.astype(F32)).astype(BF16)
    grad = after(grad, both)

    owns, theirs = {}, {}
    for mask in reversed(range(1, last)):
        part_other, owns[mask] = backward(mask, (1, 0), grad)
        theirs[mask] = swap(part_other)
        if mask == last - 1:
            gw = after(gw, owns[mask])

    halves = gw.reshape(2, -1, size, width).astype(BF16)
    kept = lax.dynamic_index_in_dim(halves, core, 0, keepdims=False)
    given = lax.dynamic_index_in_dim(halves, 1 - core, 0, keepdims=False)
    share = (kept.astype(F32) + swap(given).astype(F32)).astype(BF16)
    step = 1
    while step < n_groups:
        share = (share.astype(F32) + group(share, step).astype(F32)).astype(BF16)
        step *= 2

    if relay:
        from_ends = across(both, 1, (0, 3))
        middle = across(both, 3, (1, 2))
        from_ends = after(from_ends, middle, share, owns[1])
        far = (owns[2] + theirs[2].astype(F32) + from_ends.astype(F32)).astype(BF16)
        near = (owns[1] + theirs[1].astype(F32)).astype(BF16)
        back = after(back, far)
        far = across(jnp.concatenate([far, share]), 2)
        near = across(jnp.concatenate([near, share]), 1)
        arrived = [middle, far, near]
        shares = [share, near[row_tiles:], far[row_tiles:], across(share, 3)]
    else:
        arrived = [across(both, last)]
        for mask in reversed(range(1, last)):
            arrived.append(across((owns[mask] + theirs[mask].astype(F32)).astype(BF16), mask))
        shares = [share] + [across(share, m) for m in range(1, n_chips)]

    back_parts = [back[0]] + [group(back[k], k) for k in range(1, n_groups)]
    part_other, own_sum = call(
        functools.partial(last_products, n_groups, meta),
        "last_products",
        (jax.ShapeDtypeStruct(panel, BF16), acc_shape),
        [SMEM] * 3 + [VMEM] * (3 + n_groups),
        (VMEM, VMEM),
        [
            pltpu.VMEM((2 * row_tiles + 1, size, width), F32),
            pltpu.VMEM((n_groups * cap, size, width), BF16),
            pltpu.SMEM((n_groups,), jnp.int32),
        ],
        hubs * tile_flops,
        moved,
    )(ints, dest, hub_cols, grad, tiles[0], hub_tiles, *back_parts)
    arrived.append(swap(part_other))

    share = tree_sum([t.astype(F32) for t in shares]) * (1.0 / math.sqrt(rows_dev * n_blocks * n_groups))
    other = swap(share)
    grad_weight = jnp.concatenate(
        [jnp.where(core == 0, share, other), jnp.where(core == 0, other, share)], axis=0
    ).reshape(width, width)

    grad_feats = call(
        functools.partial(last_backward, len(arrived)),
        "last_backward",
        jax.ShapeDtypeStruct((rows_dev, width), BF16),
        [VMEM] * (2 + len(arrived)),
        VMEM,
        [],
        moved,
        moved,
    )(own_sum, *arrived, weight)
    return (layer_out.reshape(rows_dev, width), grad_feats, grad_weight)


def solution(mesh):
    in_specs = (
        P(("grp", "blk"), None),
        P(),
        P(("grp", "blk"), None),
        P(("grp", "blk")),
        P("grp", "blk", None, None, None, None),
        P("grp", "blk", None, None),
        P("grp", "blk", None, None),
        P("grp", "blk", None),
        P("grp", "blk", None, None, None),
        P("grp", "blk", None),
        P(None, "blk", None, None),
        P(None, "blk", None),
    )
    out_specs = (P(("grp", "blk"), None), P(("grp", "blk"), None), P())
    return jax.shard_map(local, mesh=mesh, in_specs=in_specs, out_specs=out_specs, check_vma=False)
```

```python
import functools
import math

import jax
import jax.numpy as jnp
from jax import lax
from jax.experimental import pallas as pl
from jax.experimental.pallas import tpu as pltpu
from jax.sharding import PartitionSpec as P

F32 = jnp.float32
BF16 = jnp.bfloat16
UNROLL = 16
SMEM = pl.BlockSpec(memory_space=pltpu.SMEM)
VMEM = pl.BlockSpec(memory_space=pltpu.VMEM)
HBM = pl.BlockSpec(memory_space=pltpu.HBM)


def dot(a, b, dims):
    return lax.dot_general(a, b, (dims, ((), ())), preferred_element_type=F32)


def call(kernel, name, out_shape, in_specs, out_specs, scratch, flops, moved, vmem=14):
    return pl.pallas_call(
        kernel,
        out_shape=out_shape,
        in_specs=in_specs,
        out_specs=out_specs,
        scratch_shapes=scratch,
        compiler_params=pltpu.CompilerParams(vmem_limit_bytes=vmem << 20),
        cost_estimate=pl.CostEstimate(flops=flops, bytes_accessed=moved, transcendentals=0),
        name=name,
    )


class Meta:
    def __init__(self, blocks, slots):
        self.slots = slots
        starts = [0]
        for size in (3, blocks, blocks * slots, blocks * slots):
            starts.append(starts[-1] + size)
        self.at = starts

    def block(self, ref, mask, other):
        chip = ref[1] ^ mask
        return 2 * chip + (ref[2] ^ 1 if other else ref[2])

    def count(self, ref, block):
        return ref[self.at[1] + block]

    def row(self, ref, block, slot):
        return ref[self.at[2] + block * self.slots + slot]

    def col(self, ref, block, slot):
        return ref[self.at[3] + block * self.slots + slot]


def stage_tiles(meta, pos, vals, *refs):
    outs, sem = refs[:-1], refs[-1]
    copies = []
    for mask, out in enumerate(outs):
        for k, side in enumerate((1, 0)):
            block = vals.at[meta.block(pos, mask, side)]
            copies.append(pltpu.make_async_copy(block, out.at[k], sem.at[2 * mask + k]))
    for copy in copies:
        copy.start()
    for copy in copies:
        copy.wait()


def tile_loop(meta, ints, mask, sides, forward, tiles, sources, total):
    blocks = [meta.block(ints, mask, side) for side in sides]
    trash = total.shape[0] - 1
    row_tiles = trash // (1 if forward else len(blocks))
    first = meta.count(ints, blocks[0])
    used = first if len(blocks) == 1 else first + meta.count(ints, blocks[1])
    contract = ((1,), (0,)) if forward else ((0,), (0,))

    def body(step, carry):
        products = []
        for u in range(UNROLL):
            at = step * UNROLL + u
            live = at < used
            if len(blocks) == 1:
                block, late, shift, slot = blocks[0], 1 - sides[0], 0, jnp.where(live, at, 0)
            else:
                late = jnp.where(at >= first, 1, 0)
                block = jnp.where(late == 1, blocks[1], blocks[0])
                shift = late * row_tiles
                slot = jnp.where(live, at - late * first, 0)
            row, col = meta.row(ints, block, slot), meta.col(ints, block, slot)
            pick, place = (col + shift, row) if forward else (row, col + shift)
            place = jnp.where(live, place, trash)
            products.append((place, dot(tiles[late, slot], sources[pick], contract)))
        for place, product in products:
            total[place] += product
        return carry

    lax.fori_loop(0, (used + UNROLL - 1) // UNROLL, body, 0)


def gather_panels(parts, panel):
    start = 0
    for part in parts:
        panel[pl.ds(start, part.shape[0])] = part[...]
        start += part.shape[0]


def forward_blocks(meta, mask, sides, has_acc, ints, *refs):
    acc, refs = (refs[0], refs[1:]) if has_acc else (None, refs)
    feats, (tiles, out, panel, total) = refs[:-4], refs[-4:]
    row_tiles = out.shape[0]
    gather_panels(feats, panel)
    if has_acc:
        total[pl.ds(0, row_tiles)] = acc[...]
    else:
        total[...] = jnp.zeros_like(total)
    tile_loop(meta, ints, mask, sides, True, tiles, panel, total)
    out[...] = total[pl.ds(0, row_tiles)]


def hub_products(groups, pos, dest, cols, feats, tiles, send, tally):
    cap = send.shape[1]
    me = pos[0]
    for k in range(groups):
        tally[k] = 0
    for h in range(tiles.shape[0]):
        to = dest[me, h] ^ me
        rank = jnp.minimum(tally[to], cap - 1)
        tally[to] = rank + 1
        send[to, rank] = dot(tiles[h], feats[cols[h]], ((1,), (0,))).astype(BF16)


def each_hub(pos, dest, groups, cap, visit):
    me = pos[0]
    for k in range(groups):
        source = me ^ k

        def body(h, rank, k=k, source=source):
            mine = dest[source, h] == me

            @pl.when(mine)
            def _():
                visit(k, source, h, jnp.minimum(rank, cap - 1))

            return rank + mine.astype(jnp.int32)

        lax.fori_loop(0, dest.shape[1], body, jnp.int32(0))


def hub_add(pos, dest, rows, *refs):
    acc, parts, out = refs[0], refs[1:-1], refs[-1]
    out[...] = acc[...]

    def visit(k, source, h, rank):
        out[rows[source, h]] += parts[k][rank].astype(F32)

    each_hub(pos, dest, len(parts), parts[0].shape[0], visit)


def last_forward(meta, mask, ints, dest, rows, acc, *refs):
    feats, refs = refs[:-9], refs[-9:]
    weight, tiles, cot, layer_out, grad, back, gw, panel, total = refs
    row_tiles = grad.shape[0]
    gather_panels(feats, panel)
    total[pl.ds(0, row_tiles)] = acc[...]
    tile_loop(meta, ints, mask, (1,), True, tiles, panel, total)
    sums = jnp.zeros(gw.shape, F32)
    for r in range(row_tiles):
        neighbours = total[r].astype(BF16)
        agg = dot(neighbours, weight[...], ((1,), (0,)))
        sig = jax.nn.sigmoid(agg)
        layer_out[r] = (agg * sig).astype(BF16)
        slope = sig * (1.0 + agg * (1.0 - sig))
        grad[r] = (cot[r].astype(F32) * slope).astype(BF16)
        sums += dot(neighbours, grad[r], ((0,), (0,)))
    gw[...] = sums

    def visit(k, source, h, rank):
        back[k, rank] = grad[rows[source, h]]

    each_hub(ints, dest, back.shape[0], back.shape[1], visit)


def backward_blocks(meta, mask, sides, ints, grad, tiles, *refs):
    parts, total = refs[:-1], refs[-1]
    row_tiles = grad.shape[0]
    total[...] = jnp.zeros_like(total)
    tile_loop(meta, ints, mask, sides, False, tiles, grad, total)
    for k, part in enumerate(parts):
        part[...] = total[pl.ds(k * row_tiles, row_tiles)].astype(part.dtype)


def last_products(groups, meta, ints, dest, cols, grad, tiles, hub_tiles, *refs):
    parts, (other, out, total, slots, tally) = refs[:groups], refs[groups:]
    row_tiles, cap = out.shape[0], parts[0].shape[0]
    me = ints[0]
    total[...] = jnp.zeros_like(total)
    tile_loop(meta, ints, 0, (1, 0), False, tiles, grad, total)
    other[...] = total[pl.ds(0, row_tiles)].astype(BF16)
    for k in range(groups):
        slots[pl.ds(k * cap, cap)] = parts[k][...]
        tally[k] = 0
    products = []
    for h in range(hub_tiles.shape[0]):
        source = dest[me, h] ^ me
        rank = jnp.minimum(tally[source], cap - 1)
        tally[source] = rank + 1
        products.append((cols[h], dot(hub_tiles[h], slots[source * cap + rank], ((0,), (0,)))))
        if len(products) == 8 or h == hub_tiles.shape[0] - 1:
            for place, product in products:
                total[row_tiles + place] += product
            products = []
    out[...] = total[pl.ds(row_tiles, row_tiles)]


def last_backward(count, *refs):
    own, parts, weight, out = refs[0], refs[1 : 1 + count], refs[-2], refs[-1]
    sums = own[...]
    for part in parts:
        sums = sums + part[pl.ds(0, own.shape[0])].astype(F32)
    out[...] = dot(sums.astype(BF16).reshape(out.shape), weight[...], ((1,), (1,))).astype(BF16)


def after(value, *others):
    return lax.optimization_barrier((value, *others))[0]


def both_sum(mine, theirs):
    return (mine.astype(F32) + theirs.astype(F32)).astype(BF16)


def local(
    feats,
    weight,
    cotangent,
    labels,
    tile_vals,
    tile_row,
    tile_col,
    tile_count,
    hub_vals,
    hub_col,
    hub_dest,
    hub_row,
):
    n_blocks = lax.axis_size("blk")
    n_groups = lax.axis_size("grp")
    n_chips = n_blocks // 2
    my_block = lax.axis_index("blk").astype(jnp.int32)
    my_group = lax.axis_index("grp").astype(jnp.int32)
    core = my_block % 2
    rows_dev, width = feats.shape
    size = tile_vals.shape[-1]
    row_tiles = rows_dev // size
    slots = tile_vals.shape[3]
    hubs = hub_vals.shape[2]
    cap = max(2, hubs // 4)
    vals = tile_vals[0, 0]
    hub_tiles = hub_vals[0, 0]
    panel = (row_tiles, size, width)
    relay = n_chips == 4
    meta = Meta(n_blocks, slots)
    pos = jnp.stack([my_group, my_block // 2, core])
    ints = jnp.concatenate([pos] + [v.reshape(-1) for v in (tile_count, tile_row, tile_col)])
    dest, hub_rows, hub_cols = hub_dest[:, 0, :, 0], hub_row[:, 0, :], hub_col[0, 0]

    def swap(value):
        return lax.ppermute(value, "blk", [(i, i ^ 1) for i in range(n_blocks)])

    def across(value, mask, chips=None):
        chosen = range(n_chips) if chips is None else chips
        pairs = [(2 * c + k, 2 * (c ^ mask) + k) for c in chosen for k in range(2)]
        return lax.ppermute(value, "blk", pairs)

    def group(value, mask):
        return lax.ppermute(value, "grp", [(i, i ^ mask) for i in range(n_groups)])

    moved, tile_flops = 100 * (4 << 20), 100 * 2 * size * size * width
    block_flops = slots * tile_flops
    acc_shape = jax.ShapeDtypeStruct(panel, F32)
    tiles = call(
        functools.partial(stage_tiles, meta),
        "stage_tiles",
        (jax.ShapeDtypeStruct((2, slots, size, size), BF16),) * n_chips,
        [SMEM, HBM],
        (VMEM,) * n_chips,
        [pltpu.SemaphoreType.DMA((n_blocks,))],
        1,
        moved,
        48,
    )(pos, vals)

    def forward(mask, sides, acc, blocks):
        return call(
            functools.partial(forward_blocks, meta, mask, sides, acc is not None),
            "forward_blocks",
            acc_shape,
            [SMEM] + [VMEM] * (len(blocks) + (1 if acc is None else 2)),
            VMEM,
            [
                pltpu.VMEM((len(sides) * row_tiles, size, width), BF16),
                pltpu.VMEM((row_tiles + 1, size, width), F32),
            ],
            len(sides) * block_flops,
            moved,
        )(ints, *(() if acc is None else (acc,)), *blocks, tiles[mask])

    def backward(mask, sides, grad):
        return call(
            functools.partial(backward_blocks, meta, mask, sides),
            "backward_blocks",
            tuple(jax.ShapeDtypeStruct(panel, BF16 if side else F32) for side in sides),
            [SMEM, VMEM, VMEM],
            (VMEM,) * len(sides),
            [
                pltpu.VMEM((len(sides) * row_tiles + 1, size, width), F32),
            ],
            len(sides) * block_flops,
            moved,
        )(ints, grad, tiles[mask])

    last = n_chips - 1
    feats = feats.reshape(panel)
    got, pairs = {0: [feats]}, {0: [swap(feats)]}
    if relay:
        got[2] = [across(feats, 2)]
        got[1] = [across(feats, 1)]
    else:
        for mask in range(1, n_chips):
            got[mask] = [across(feats, mask)]

    send = call(
        functools.partial(hub_products, n_groups),
        "hub_products",
        jax.ShapeDtypeStruct((n_groups, cap, size, width), BF16),
        [SMEM, SMEM, SMEM, VMEM, VMEM],
        VMEM,
        [pltpu.SMEM((n_groups,), jnp.int32)],
        hubs * tile_flops,
        moved,
    )(pos, dest, hub_cols, after(feats, *pairs[0]), hub_tiles)
    hub_parts = [send[0]] + [group(send[k], k) for k in range(1, n_groups)]
    acc = forward(0, (1, 0), None, (*pairs[0], *got[0]))
    if relay:
        passed = across(after(got[2][0], acc), 1, (1, 2))
        direct = across(after(feats, acc, got[2][0]), 3, (1, 2))
    acc = call(
        hub_add,
        "hub_add",
        acc_shape,
        [SMEM] * 3 + [VMEM] * (1 + n_groups),
        VMEM,
        [],
        1 << 20,
        moved,
    )(pos, dest, hub_rows, acc, *hub_parts)
    for mask in range(1, last):
        pairs[mask] = [swap(part) for part in got[mask]]
        acc = forward(mask, (1, 0), acc, (*pairs[mask], *got[mask]))
    if relay:
        got[last] = [after(passed, acc) + direct]
    pairs[last] = [swap(part) for part in got[last]]
    acc = forward(last, (0,), acc, got[last])

    cot = jnp.where(labels[:, None] >= 0, cotangent, jnp.zeros_like(cotangent)).reshape(panel)
    layer_out, grad, back, gw = call(
        functools.partial(last_forward, meta, last),
        "last_forward",
        (
            jax.ShapeDtypeStruct(panel, BF16),
            jax.ShapeDtypeStruct(panel, BF16),
            jax.ShapeDtypeStruct((n_groups, cap, size, width), BF16),
            jax.ShapeDtypeStruct((width, width), F32),
        ),
        [SMEM] * 3 + [VMEM] * (4 + len(pairs[last])),
        (VMEM,) * 4,
        [
            pltpu.VMEM(panel, BF16),
            pltpu.VMEM((row_tiles + 1, size, width), F32),
        ],
        block_flops,
        moved,
    )(ints, dest, hub_rows, acc, *pairs[last], weight, tiles[last], cot)

    (part_other,) = backward(last, (1,), grad)
    theirs = swap(part_other)
    (part_own,) = backward(last, (0,), grad)
    both = (part_own + theirs.astype(F32)).astype(BF16)
    grad = after(grad, both)

    gw = after(gw, both)
    halves = gw.reshape(2, -1, size, width).astype(BF16)
    kept = lax.dynamic_index_in_dim(halves, core, 0, keepdims=False)
    given = lax.dynamic_index_in_dim(halves, 1 - core, 0, keepdims=False)
    share = both_sum(kept, swap(given))
    step = 1
    while step < n_groups:
        share = both_sum(share, group(share, step))
        step *= 2

    owns, theirs = {}, {}
    for mask in reversed(range(1, last)):
        part_other, owns[mask] = backward(mask, (1, 0), grad)
        theirs[mask] = swap(part_other)
    if relay:
        from_ends = across(both, 1, (0, 3))
        middle = across(both, 3, (1, 2))
        from_ends = after(from_ends, middle, owns[1])
        far = (owns[2] + theirs[2].astype(F32) + from_ends.astype(F32)).astype(BF16)
        near = (owns[1] + theirs[1].astype(F32)).astype(BF16)
        near = after(near, far)
        arrived = [middle, across(far, 2), across(near, 1)]
    else:
        arrived = [across(both, last)]
        for mask in reversed(range(1, last)):
            arrived.append(across((owns[mask] + theirs[mask].astype(F32)).astype(BF16), mask))
    for step in tuple(m for m in (2, 1) if m < n_chips) + tuple(1 << i for i in range(2, 8) if 1 << i < n_chips):
        share = both_sum(share, across(share, step))

    parts = [back[k] for k in range(n_groups)]
    step = 1
    while step < n_groups:
        chosen = [k for k in range(n_groups) if k & step]
        sent = jnp.concatenate([parts[k] for k in chosen])
        if step == 1:
            sent = after(sent, both)
        elif relay and step == 2:
            sent = after(sent, far)
        moved_parts = group(sent, step)
        for i, k in enumerate(chosen):
            parts[k] = moved_parts[i * cap : (i + 1) * cap]
        step *= 2
    part_other, own_sum = call(
        functools.partial(last_products, n_groups, meta),
        "last_products",
        (jax.ShapeDtypeStruct(panel, BF16), acc_shape),
        [SMEM] * 3 + [VMEM] * (3 + n_groups),
        (VMEM, VMEM),
        [
            pltpu.VMEM((2 * row_tiles + 1, size, width), F32),
            pltpu.VMEM((n_groups * cap, size, width), BF16),
            pltpu.SMEM((n_groups,), jnp.int32),
        ],
        hubs * tile_flops,
        moved,
    )(ints, dest, hub_cols, grad, tiles[0], hub_tiles, *parts)
    arrived.append(swap(part_other))

    share = share.astype(F32) * (1.0 / math.sqrt(rows_dev * n_blocks * n_groups))
    other = swap(share)
    grad_weight = jnp.concatenate(
        [jnp.where(core == 0, share, other), jnp.where(core == 0, other, share)], axis=0
    ).reshape(width, width)

    grad_feats = call(
        functools.partial(last_backward, len(arrived)),
        "last_backward",
        jax.ShapeDtypeStruct((rows_dev, width), BF16),
        [VMEM] * (2 + len(arrived)),
        VMEM,
        [],
        moved,
        moved,
    )(own_sum, *arrived, weight)
    return (layer_out.reshape(rows_dev, width), grad_feats, grad_weight)


def solution(mesh):
    in_specs = (
        P(("grp", "blk"), None),
        P(),
        P(("grp", "blk"), None),
        P(("grp", "blk")),
        P("grp", "blk", None, None, None, None),
        P("grp", "blk", None, None),
        P("grp", "blk", None, None),
        P("grp", "blk", None),
        P("grp", "blk", None, None, None),
        P("grp", "blk", None),
        P(None, "blk", None, None),
        P(None, "blk", None),
    )
    out_specs = (P(("grp", "blk"), None), P(("grp", "blk"), None), P())
    return jax.shard_map(local, mesh=mesh, in_specs=in_specs, out_specs=out_specs, check_vma=False)
```

```python
import functools
import math

import jax
import jax.numpy as jnp
from jax import lax
from jax.experimental import pallas as pl
from jax.experimental.pallas import tpu as pltpu
from jax.sharding import PartitionSpec as P

F32 = jnp.float32
BF16 = jnp.bfloat16
UNROLL = 16
SMEM = pl.BlockSpec(memory_space=pltpu.SMEM)
VMEM = pl.BlockSpec(memory_space=pltpu.VMEM)
HBM = pl.BlockSpec(memory_space=pltpu.HBM)


def dot(a, b, dims):
    return lax.dot_general(a, b, (dims, ((), ())), preferred_element_type=F32)


def call(kernel, name, out_shape, in_specs, out_specs, scratch, flops, moved, vmem=14):
    return pl.pallas_call(
        kernel,
        out_shape=out_shape,
        in_specs=in_specs,
        out_specs=out_specs,
        scratch_shapes=scratch,
        compiler_params=pltpu.CompilerParams(vmem_limit_bytes=vmem << 20),
        cost_estimate=pl.CostEstimate(flops=flops, bytes_accessed=moved, transcendentals=0),
        name=name,
    )


class Meta:
    def __init__(self, blocks, slots):
        self.slots = slots
        starts = [0]
        for size in (3, blocks, blocks * slots, blocks * slots):
            starts.append(starts[-1] + size)
        self.at = starts

    def block(self, ref, mask, other):
        chip = ref[1] ^ mask
        return 2 * chip + (ref[2] ^ 1 if other else ref[2])

    def count(self, ref, block):
        return ref[self.at[1] + block]

    def row(self, ref, block, slot):
        return ref[self.at[2] + block * self.slots + slot]

    def col(self, ref, block, slot):
        return ref[self.at[3] + block * self.slots + slot]


def stage_tiles(meta, pos, vals, *refs):
    outs, sem = refs[:-1], refs[-1]
    copies = []
    for mask, out in enumerate(outs):
        for k, side in enumerate((1, 0)):
            block = vals.at[meta.block(pos, mask, side)]
            copies.append(pltpu.make_async_copy(block, out.at[k], sem.at[2 * mask + k]))
    for copy in copies:
        copy.start()
    for copy in copies:
        copy.wait()


def tile_loop(meta, ints, mask, sides, forward, tiles, sources, total):
    blocks = [meta.block(ints, mask, side) for side in sides]
    trash = total.shape[0] - 1
    row_tiles = trash // (1 if forward else len(blocks))
    first = meta.count(ints, blocks[0])
    used = first if len(blocks) == 1 else first + meta.count(ints, blocks[1])
    contract = ((1,), (0,)) if forward else ((0,), (0,))

    def body(step, carry):
        products = []
        for u in range(UNROLL):
            at = step * UNROLL + u
            live = at < used
            if len(blocks) == 1:
                block, late, shift, slot = blocks[0], 1 - sides[0], 0, jnp.where(live, at, 0)
            else:
                late = jnp.where(at >= first, 1, 0)
                block = jnp.where(late == 1, blocks[1], blocks[0])
                shift = late * row_tiles
                slot = jnp.where(live, at - late * first, 0)
            row, col = meta.row(ints, block, slot), meta.col(ints, block, slot)
            pick, place = (col + shift, row) if forward else (row, col + shift)
            place = jnp.where(live, place, trash)
            products.append((place, dot(tiles[late, slot], sources[pick], contract)))
        for place, product in products:
            total[place] += product
        return carry

    lax.fori_loop(0, (used + UNROLL - 1) // UNROLL, body, 0)


def gather_panels(parts, panel):
    start = 0
    for part in parts:
        panel[pl.ds(start, part.shape[0])] = part[...]
        start += part.shape[0]


def forward_blocks(meta, mask, sides, has_acc, ints, *refs):
    acc, refs = (refs[0], refs[1:]) if has_acc else (None, refs)
    feats, (tiles, out, panel, total) = refs[:-4], refs[-4:]
    row_tiles = out.shape[0]
    gather_panels(feats, panel)
    if has_acc:
        total[pl.ds(0, row_tiles)] = acc[...]
    else:
        total[...] = jnp.zeros_like(total)
    tile_loop(meta, ints, mask, sides, True, tiles, panel, total)
    out[...] = total[pl.ds(0, row_tiles)]


def hub_products(groups, pos, dest, cols, feats, tiles, send, tally):
    cap = send.shape[1]
    me = pos[0]
    for k in range(groups):
        tally[k] = 0
    for h in range(tiles.shape[0]):
        to = dest[me, h] ^ me
        rank = jnp.minimum(tally[to], cap - 1)
        tally[to] = rank + 1
        send[to, rank] = dot(tiles[h], feats[cols[h]], ((1,), (0,))).astype(BF16)


def each_hub(pos, dest, groups, cap, visit):
    me = pos[0]
    for k in range(groups):
        source = me ^ k

        def body(h, rank, k=k, source=source):
            mine = dest[source, h] == me

            @pl.when(mine)
            def _():
                visit(k, source, h, jnp.minimum(rank, cap - 1))

            return rank + mine.astype(jnp.int32)

        lax.fori_loop(0, dest.shape[1], body, jnp.int32(0))


def hub_add(pos, dest, rows, *refs):
    acc, parts, out = refs[0], refs[1:-1], refs[-1]
    out[...] = acc[...]

    def visit(k, source, h, rank):
        out[rows[source, h]] += parts[k][rank].astype(F32)

    each_hub(pos, dest, len(parts), parts[0].shape[0], visit)


def last_forward(meta, mask, ints, dest, rows, acc, *refs):
    feats, refs = refs[:-9], refs[-9:]
    weight, tiles, cot, layer_out, grad, back, gw, panel, total = refs
    row_tiles = grad.shape[0]
    gather_panels(feats, panel)
    total[pl.ds(0, row_tiles)] = acc[...]
    tile_loop(meta, ints, mask, (1,), True, tiles, panel, total)
    sums = jnp.zeros(gw.shape, F32)
    for r in range(row_tiles):
        neighbours = total[r].astype(BF16)
        agg = dot(neighbours, weight[...], ((1,), (0,)))
        sig = jax.nn.sigmoid(agg)
        layer_out[r] = (agg * sig).astype(BF16)
        slope = sig * (1.0 + agg * (1.0 - sig))
        grad[r] = (cot[r].astype(F32) * slope).astype(BF16)
        sums += dot(neighbours, grad[r], ((0,), (0,)))
    gw[...] = sums

    def visit(k, source, h, rank):
        back[k, rank] = grad[rows[source, h]]

    each_hub(ints, dest, back.shape[0], back.shape[1], visit)


def backward_blocks(meta, mask, sides, ints, grad, tiles, *refs):
    parts, total = refs[:-1], refs[-1]
    row_tiles = grad.shape[0]
    total[...] = jnp.zeros_like(total)
    tile_loop(meta, ints, mask, sides, False, tiles, grad, total)
    for k, part in enumerate(parts):
        part[...] = total[pl.ds(k * row_tiles, row_tiles)].astype(part.dtype)


def last_products(groups, meta, ints, dest, cols, grad, tiles, hub_tiles, *refs):
    parts, (other, out, total, slots, tally) = refs[:groups], refs[groups:]
    row_tiles, cap = out.shape[0], parts[0].shape[0]
    me = ints[0]
    total[...] = jnp.zeros_like(total)
    tile_loop(meta, ints, 0, (1, 0), False, tiles, grad, total)
    other[...] = total[pl.ds(0, row_tiles)].astype(BF16)
    for k in range(groups):
        slots[pl.ds(k * cap, cap)] = parts[k][...]
        tally[k] = 0
    products = []
    for h in range(hub_tiles.shape[0]):
        source = dest[me, h] ^ me
        rank = jnp.minimum(tally[source], cap - 1)
        tally[source] = rank + 1
        products.append((cols[h], dot(hub_tiles[h], slots[source * cap + rank], ((0,), (0,)))))
        if len(products) == 8 or h == hub_tiles.shape[0] - 1:
            for place, product in products:
                total[row_tiles + place] += product
            products = []
    out[...] = total[pl.ds(row_tiles, row_tiles)]


def last_backward(count, *refs):
    own, parts, weight, out = refs[0], refs[1 : 1 + count], refs[-2], refs[-1]
    sums = own[...]
    for part in parts:
        sums = sums + part[pl.ds(0, own.shape[0])].astype(F32)
    out[...] = dot(sums.astype(BF16).reshape(out.shape), weight[...], ((1,), (1,))).astype(BF16)


def after(value, *others):
    return lax.optimization_barrier((value, *others))[0]


def both_sum(mine, theirs):
    return (mine.astype(F32) + theirs.astype(F32)).astype(BF16)


def local(
    feats,
    weight,
    cotangent,
    labels,
    tile_vals,
    tile_row,
    tile_col,
    tile_count,
    hub_vals,
    hub_col,
    hub_dest,
    hub_row,
):
    n_blocks = lax.axis_size("blk")
    n_groups = lax.axis_size("grp")
    n_chips = n_blocks // 2
    my_block = lax.axis_index("blk").astype(jnp.int32)
    my_group = lax.axis_index("grp").astype(jnp.int32)
    core = my_block % 2
    rows_dev, width = feats.shape
    size = tile_vals.shape[-1]
    row_tiles = rows_dev // size
    slots = tile_vals.shape[3]
    hubs = hub_vals.shape[2]
    cap = max(2, hubs // 4)
    vals = tile_vals[0, 0]
    hub_tiles = hub_vals[0, 0]
    panel = (row_tiles, size, width)
    relay = n_chips == 4
    meta = Meta(n_blocks, slots)
    pos = jnp.stack([my_group, my_block // 2, core])
    ints = jnp.concatenate([pos] + [v.reshape(-1) for v in (tile_count, tile_row, tile_col)])
    dest, hub_rows, hub_cols = hub_dest[:, 0, :, 0], hub_row[:, 0, :], hub_col[0, 0]

    def swap(value):
        return lax.ppermute(value, "blk", [(i, i ^ 1) for i in range(n_blocks)])

    def across(value, mask, chips=None):
        chosen = range(n_chips) if chips is None else chips
        pairs = [(2 * c + k, 2 * (c ^ mask) + k) for c in chosen for k in range(2)]
        return lax.ppermute(value, "blk", pairs)

    def group(value, mask):
        return lax.ppermute(value, "grp", [(i, i ^ mask) for i in range(n_groups)])

    moved, tile_flops = 100 * (4 << 20), 100 * 2 * size * size * width
    block_flops = slots * tile_flops
    acc_shape = jax.ShapeDtypeStruct(panel, F32)
    tiles = call(
        functools.partial(stage_tiles, meta),
        "stage_tiles",
        (jax.ShapeDtypeStruct((2, slots, size, size), BF16),) * n_chips,
        [SMEM, HBM],
        (VMEM,) * n_chips,
        [pltpu.SemaphoreType.DMA((n_blocks,))],
        1,
        moved,
        48,
    )(pos, vals)

    def forward(mask, sides, acc, blocks):
        return call(
            functools.partial(forward_blocks, meta, mask, sides, acc is not None),
            "forward_blocks",
            acc_shape,
            [SMEM] + [VMEM] * (len(blocks) + (1 if acc is None else 2)),
            VMEM,
            [
                pltpu.VMEM((len(sides) * row_tiles, size, width), BF16),
                pltpu.VMEM((row_tiles + 1, size, width), F32),
            ],
            len(sides) * block_flops,
            moved,
        )(ints, *(() if acc is None else (acc,)), *blocks, tiles[mask])

    def backward(mask, sides, grad):
        return call(
            functools.partial(backward_blocks, meta, mask, sides),
            "backward_blocks",
            tuple(jax.ShapeDtypeStruct(panel, BF16 if side else F32) for side in sides),
            [SMEM, VMEM, VMEM],
            (VMEM,) * len(sides),
            [
                pltpu.VMEM((len(sides) * row_tiles + 1, size, width), F32),
            ],
            len(sides) * block_flops,
            moved,
        )(ints, grad, tiles[mask])

    last = n_chips - 1
    feats = feats.reshape(panel)
    got, pairs = {0: [feats]}, {0: [swap(feats)]}
    if relay:
        got[2] = [across(feats, 2)]
        got[1] = [across(feats, 1)]
    else:
        for mask in range(1, n_chips):
            got[mask] = [across(feats, mask)]

    send = call(
        functools.partial(hub_products, n_groups),
        "hub_products",
        jax.ShapeDtypeStruct((n_groups, cap, size, width), BF16),
        [SMEM, SMEM, SMEM, VMEM, VMEM],
        VMEM,
        [pltpu.SMEM((n_groups,), jnp.int32)],
        hubs * tile_flops,
        moved,
    )(pos, dest, hub_cols, after(feats, *pairs[0]), hub_tiles)
    hub_parts = [send[0]] + [group(send[k], k) for k in range(1, n_groups)]
    acc = forward(0, (1, 0), None, (*pairs[0], *got[0]))
    if relay:
        passed = across(after(got[2][0], acc), 1, (1, 2))
        direct = across(after(feats, acc, got[2][0]), 3, (1, 2))
    acc = call(
        hub_add,
        "hub_add",
        acc_shape,
        [SMEM] * 3 + [VMEM] * (1 + n_groups),
        VMEM,
        [],
        1 << 20,
        moved,
    )(pos, dest, hub_rows, acc, *hub_parts)
    for mask in range(1, last):
        pairs[mask] = [swap(part) for part in got[mask]]
        acc = forward(mask, (1, 0), acc, (*pairs[mask], *got[mask]))
    if relay:
        got[last] = [after(passed, acc) + direct]
    pairs[last] = [swap(part) for part in got[last]]
    acc = forward(last, (0,), acc, got[last])

    cot = jnp.where(labels[:, None] >= 0, cotangent, jnp.zeros_like(cotangent)).reshape(panel)
    layer_out, grad, back, gw = call(
        functools.partial(last_forward, meta, last),
        "last_forward",
        (
            jax.ShapeDtypeStruct(panel, BF16),
            jax.ShapeDtypeStruct(panel, BF16),
            jax.ShapeDtypeStruct((n_groups, cap, size, width), BF16),
            jax.ShapeDtypeStruct((width, width), F32),
        ),
        [SMEM] * 3 + [VMEM] * (4 + len(pairs[last])),
        (VMEM,) * 4,
        [
            pltpu.VMEM(panel, BF16),
            pltpu.VMEM((row_tiles + 1, size, width), F32),
        ],
        block_flops,
        moved,
    )(ints, dest, hub_rows, acc, *pairs[last], weight, tiles[last], cot)

    (part_other,) = backward(last, (1,), grad)
    theirs = swap(part_other)
    (part_own,) = backward(last, (0,), grad)
    both = (part_own + theirs.astype(F32)).astype(BF16)
    grad = after(grad, both)

    gw = after(gw, both)
    halves = gw.reshape(2, -1, size, width).astype(BF16)
    kept = lax.dynamic_index_in_dim(halves, core, 0, keepdims=False)
    given = lax.dynamic_index_in_dim(halves, 1 - core, 0, keepdims=False)
    share = both_sum(kept, swap(given))
    step = 1
    while step < n_groups:
        share = both_sum(share, group(share, step))
        step *= 2

    owns, theirs = {}, {}
    for mask in reversed(range(1, last)):
        part_other, owns[mask] = backward(mask, (1, 0), grad)
        theirs[mask] = swap(part_other)
    if relay:
        from_ends = across(both, 1, (0, 3))
        middle = across(both, 3, (1, 2))
        from_ends = after(from_ends, middle, owns[1])
        far = (owns[2] + theirs[2].astype(F32) + from_ends.astype(F32)).astype(BF16)
        near = (owns[1] + theirs[1].astype(F32)).astype(BF16)
        arrived = [middle, across(far, 2), across(near, 1)]
    else:
        arrived = [across(both, last)]
        for mask in reversed(range(1, last)):
            arrived.append(across((owns[mask] + theirs[mask].astype(F32)).astype(BF16), mask))
    for step in tuple(m for m in (2, 1) if m < n_chips) + tuple(1 << i for i in range(2, 8) if 1 << i < n_chips):
        share = both_sum(share, across(share, step))

    parts = [back[k] for k in range(n_groups)]
    step = 1
    while step < n_groups:
        chosen = [k for k in range(n_groups) if k & step]
        sent = jnp.concatenate([parts[k] for k in chosen])
        if relay and step == 1:
            sent = after(sent, theirs[2])
        elif relay and step == 2:
            sent = after(sent, far)
        moved_parts = group(sent, step)
        for i, k in enumerate(chosen):
            parts[k] = moved_parts[i * cap : (i + 1) * cap]
        step *= 2
    part_other, own_sum = call(
        functools.partial(last_products, n_groups, meta),
        "last_products",
        (jax.ShapeDtypeStruct(panel, BF16), acc_shape),
        [SMEM] * 3 + [VMEM] * (3 + n_groups),
        (VMEM, VMEM),
        [
            pltpu.VMEM((2 * row_tiles + 1, size, width), F32),
            pltpu.VMEM((n_groups * cap, size, width), BF16),
            pltpu.SMEM((n_groups,), jnp.int32),
        ],
        hubs * tile_flops,
        moved,
    )(ints, dest, hub_cols, grad, tiles[0], hub_tiles, *parts)
    arrived.append(swap(part_other))

    share = share.astype(F32) * (1.0 / math.sqrt(rows_dev * n_blocks * n_groups))
    other = swap(share)
    grad_weight = jnp.concatenate(
        [jnp.where(core == 0, share, other), jnp.where(core == 0, other, share)], axis=0
    ).reshape(width, width)

    grad_feats = call(
        functools.partial(last_backward, len(arrived)),
        "last_backward",
        jax.ShapeDtypeStruct((rows_dev, width), BF16),
        [VMEM] * (2 + len(arrived)),
        VMEM,
        [],
        moved,
        moved,
    )(own_sum, *arrived, weight)
    return (layer_out.reshape(rows_dev, width), grad_feats, grad_weight)


def solution(mesh):
    in_specs = (
        P(("grp", "blk"), None),
        P(),
        P(("grp", "blk"), None),
        P(("grp", "blk")),
        P("grp", "blk", None, None, None, None),
        P("grp", "blk", None, None),
        P("grp", "blk", None, None),
        P("grp", "blk", None),
        P("grp", "blk", None, None, None),
        P("grp", "blk", None),
        P(None, "blk", None, None),
        P(None, "blk", None),
    )
    out_specs = (P(("grp", "blk"), None), P(("grp", "blk"), None), P())
    return jax.shard_map(local, mesh=mesh, in_specs=in_specs, out_specs=out_specs, check_vma=False)
```
